32 devices in a mesh: space: 4 (over z), tm: 4 (over y, x), param: 2 (over core).
Axes of the slice: x: 2, y: 2, z: 4, core: 2. Of those that a mesh axis runs over, the one named last changes fastest.
Arguments:
- snapshots: float32 [512, 64, 3072], P('tm', 'param', 'space'), may hold values from -6 to 6
- time_basis: float32 [512, 64], replicated, may hold values from -0.25 to 0.25
Outputs:
- gram_time: float32 [512, 512], P('tm')
- core: float32 [64, 64, 3072], P('tm', 'param', 'space')
- gram_param: float32 [64, 64], P('param')
The draws below stay inside these ranges and needn't reach their ends.
All inputs are finite; a program needn't handle non-finite values.
Results may differ from the reference program's by a relative error of at most 0.000071.
Values sent between devices are 32-bit elements; how exact they have to be, the bound alone decides.
No kernel may reach another device: no remote copies, remote signals or barrier semaphores. Data moves between devices by JAX's collectives and lax.ppermute only.
A program may use at most 128 MiB of HBM per device.

```python
import jax
import jax.numpy as jnp
from jax import lax

TT = 512
RANK = 64
LOADS = 64
POINTS = 3072


def block_scale(own_key, shape, cuts, least, top_value):
    def one(dim, blocks):
        steps = jax.random.uniform(jax.random.fold_in(jax.random.fold_in(own_key, 6), dim), (blocks,), jnp.float32, least / len(cuts), top_value / len(cuts))
        return jnp.repeat(jnp.exp(steps), shape[dim] // blocks).reshape((-1,) + (1,) * (len(shape) - dim - 1))

    loudness = one(*cuts[0])
    for cut in cuts[1:]:
        loudness = loudness * one(*cut)
    return loudness


def gaussian(own_key, extent, spread, limit, pieces=(), held_as=jnp.bfloat16):
    values = spread * jax.random.normal(own_key, extent, jnp.float32)
    if pieces:
        values = values * block_scale(own_key, extent, pieces, -0.22, 0.18)
    return jnp.clip(values, -limit, limit).astype(held_as)


def setup_inputs(seed: int = 0) -> dict:
    streams_of = jax.random.split(jax.random.key(seed), 3)
    snapshots = gaussian(streams_of[0], (TT, LOADS, POINTS), 1.0, 6.0, ((0, 4), (1, 2), (2, 4)), jnp.float32)
    time_basis = gaussian(streams_of[1], (TT, RANK), TT ** -0.5, 0.25, (), jnp.float32)
    return {"snapshots": snapshots, "time_basis": time_basis}


def reference(snapshots, time_basis):
    flat = snapshots.reshape(TT, LOADS * POINTS)
    gram_time = jnp.dot(flat, flat.T, precision=lax.Precision.HIGHEST, preferred_element_type=jnp.float32) / (LOADS * POINTS)
    core_flat = jnp.dot(time_basis.T, flat, precision=lax.Precision.HIGHEST, preferred_element_type=jnp.float32)
    core = core_flat.reshape(RANK, LOADS, POINTS)
    gram_param = jnp.einsum("rps,rqs->pq", core, core, precision=lax.Precision.HIGHEST) / (RANK * POINTS)
    return gram_time, core, gram_param
```

```python
import functools

import jax
import jax.numpy as jnp
from jax import lax
from jax.experimental import pallas as pl
from jax.experimental.pallas import tpu as pltpu
from jax.sharding import PartitionSpec as P

LANES = 128
precise_mode = lax.Precision.HIGHEST


def xor_pairs(k, n):
    return [(i, i ^ k) for i in range(n)]


def swap(v, axis, k):
    return lax.ppermute(v, axis, xor_pairs(k, lax.axis_size(axis)))


def all_sum(v, axis):
    k = 1
    while k < lax.axis_size(axis):
        v = v + swap(v, axis, k)
        k *= 2
    return v


def all_sum_direct(v, axis):
    parts = [swap(v, axis, k) for k in range(1, lax.axis_size(axis))]
    for part in parts:
        v = v + part
    return v


def split(v):
    high = v.astype(jnp.bfloat16)
    return high, (v - high.astype(jnp.float32)).astype(jnp.bfloat16)


def dot_t(a, b):
    return lax.dot_general(
        a, b, (((1,), (1,)), ((), ())), preferred_element_type=jnp.float32
    )


def pack_kernel(n, place, *refs):
    for share, packed in zip(refs[:n], refs[n:]):
        for p in range(share.shape[1]):
            packed[p] = share[:, p, :]


def pack(place, snapshots, chunk, n, cut, group):
    rows = snapshots.shape[0]
    width = cut if chunk[0] == "load" else group
    part = 32 if rows % 32 == 0 else rows

    def spec(k):
        if chunk[0] == "load":
            where = lambda i, place: (i, place[0] ^ k, chunk[1])
        else:
            where = lambda i, place: (i, chunk[2], chunk[1] * n + (place[0] ^ k))
        return pl.BlockSpec((part, width, LANES), where)

    return pl.pallas_call(
        functools.partial(pack_kernel, n),
        out_shape=[jax.ShapeDtypeStruct((width, rows, LANES), jnp.float32)] * n,
        grid_spec=pltpu.PrefetchScalarGridSpec(
            num_scalar_prefetch=1,
            grid=(rows // part,),
            in_specs=[spec(k) for k in range(n)],
            out_specs=[pl.BlockSpec((width, part, LANES), lambda i, place: (0, i, 0))]
            * n,
        ),
        cost_estimate=pl.CostEstimate(
            flops=0, bytes_accessed=8 * n * width * rows * LANES, transcendentals=0
        ),
    )(place, *[snapshots] * n)


def chunk_kernel(n, first, last, pair, place, basis, *refs):
    blocks, refs = refs[:n], refs[n:]
    if not first:
        before, refs = refs[0], refs[1:]
    core, pieces, refs = refs[0], refs[1:n], refs[n:]
    if last:
        keep, send, total, high, low = refs
    else:
        total, high, low = refs
    step = pl.program_id(0)
    steps = high.shape[0]
    me, half = place[0], place[1]
    rows = blocks[0].shape[1]
    rank = core.shape[0]
    for e in range(pair):
        for k in range(n):
            h, l = split(blocks[k][e])
            at = pl.ds(pl.multiple_of((me ^ k) * rows, rows), rows)
            high[step, at, e * LANES : (e + 1) * LANES] = h
            low[step, at, e * LANES : (e + 1) * LANES] = l

    @pl.when(step == steps - 1)
    def _():
        h = jnp.concatenate([high[s] for s in range(steps)], axis=1)
        l = jnp.concatenate([low[s] for s in range(steps)], axis=1)
        product = dot_t(
            jnp.concatenate([h, h, l], axis=1), jnp.concatenate([h, l, h], axis=1)
        )
        if first:
            total[...] = product
        else:
            total[...] = before[...] + product
        if last:
            cut = keep.shape[1]
            for j in range(n):
                mine = pl.multiple_of(j * rows + half * cut, cut)
                other = pl.multiple_of(j * rows + (1 - half) * cut, cut)
                keep[j] = total[pl.ds(mine, cut), :]
                send[j] = total[pl.ds(other, cut), :]
        b = jnp.concatenate(split(basis[...]), axis=0)
        wide = jnp.dot(b, h, preferred_element_type=jnp.float32)
        wide = wide + jnp.dot(b, l, preferred_element_type=jnp.float32)
        values = wide[:rank] + wide[rank:]
        own = rank // n
        for p in range(core.shape[1]):
            part = values[:, p * LANES : (p + 1) * LANES]
            core[:, p, :] = part
            for k in range(1, n):
                pieces[k - 1][:, p, :] = part[k * own : (k + 1) * own]


def run_chunk(place, basis, blocks, before, last):
    n = len(blocks)
    loads, rows, lanes = blocks[0].shape
    steps = n * rows
    rank = basis.shape[0]
    pair = 2 if loads % 2 == 0 else 1
    first = before is None
    whole = lambda *dims: pl.BlockSpec(dims, lambda i, place: (0,) * len(dims))
    in_specs = [whole(*basis.shape)]
    in_specs += [pl.BlockSpec((pair, rows, lanes), lambda i, place: (i, 0, 0))] * n
    args = [place, basis, *blocks]
    if not first:
        in_specs.append(whole(steps, steps))
        args.append(before)
    f32 = lambda *dims: jax.ShapeDtypeStruct(dims, jnp.float32)
    shapes = [f32(rank, loads, lanes)] + [f32(rank // n, loads, lanes)] * (n - 1)
    scratch = [pltpu.VMEM((loads // pair, steps, pair * lanes), jnp.bfloat16)] * 2
    if last:
        shapes += [f32(n, rows // 2, steps)] * 2
        scratch = [pltpu.VMEM((steps, steps), jnp.float32)] + scratch
    else:
        shapes += [f32(steps, steps)]
    points = loads * lanes
    return pl.pallas_call(
        functools.partial(chunk_kernel, n, first, last, pair),
        out_shape=shapes,
        grid_spec=pltpu.PrefetchScalarGridSpec(
            num_scalar_prefetch=1,
            grid=(loads // pair,),
            in_specs=in_specs,
            out_specs=[whole(*s.shape) for s in shapes],
            scratch_shapes=scratch,
        ),
        compiler_params=pltpu.CompilerParams(vmem_limit_bytes=40 * 2**20),
        cost_estimate=pl.CostEstimate(
            flops=2 * steps * points * (3 * steps + 4 * rank),
            bytes_accessed=4 * steps * (points + 2 * steps),
            transcendentals=0,
        ),
    )(*args)


def body(snapshots, time_basis):
    rows, loads, points = snapshots.shape
    n = lax.axis_size("tm")
    me, half = lax.axis_index("tm"), lax.axis_index("param")
    rank = time_basis.shape[1]
    own_rank = rank // n
    total_points = points * lax.axis_size("space")
    total_loads = loads * lax.axis_size("param")
    tiles = points // LANES
    cut = loads // n
    mains = tiles // n
    group = 8 if loads % 8 == 0 else loads

    chunks = [("load", t) for t in range(mains * n, tiles)]
    chunks += [("tile", m, g) for m in range(mains) for g in range(loads // group)]

    place = jnp.stack([me, half]).astype(jnp.int32)
    order = me ^ jnp.arange(n)
    basis = time_basis.reshape(-1, n, own_rank)[:, order].reshape(-1, rank).T

    def shares(x, chunk):
        if (cut if chunk[0] == "load" else group) % 8 == 0:
            return pack(place, x, chunk, n, cut, group)
        out = []
        for k in range(n):
            j = me ^ k
            if chunk[0] == "load":
                start, size = (0, j * cut, chunk[1] * LANES), (rows, cut, LANES)
            else:
                start = (0, chunk[2] * group, (chunk[1] * n + j) * LANES)
                size = (rows, group, LANES)
            out.append(lax.dynamic_slice(x, start, size).transpose(1, 0, 2))
        return out

    held = []
    for i, chunk in enumerate(chunks):
        x = snapshots
        if i >= 2:
            x = lax.optimization_barrier((x, held[i - 2][1:]))[0]
        parts = shares(x, chunk)
        held.append([parts[0]] + [swap(parts[k], "tm", k) for k in range(1, n)])

    total = None
    cores, pieces = [], []
    for i, chunk in enumerate(chunks):
        last = i == len(chunks) - 1
        out = run_chunk(place, basis, held[i], total, last)
        cores.append(out[0])
        pieces.append(out[1:n])
        total = out[n]
        if last:
            keep, send = out[n], out[n + 1]

    rows_part = keep + swap(send, "param", 1)
    pick = lambda v, k: lax.dynamic_index_in_dim(v, me ^ k, 0, False)
    arrived = [swap(pick(rows_part, k), "tm", k) for k in range(1, n)]
    mine = pick(rows_part, 0)
    for part in arrived:
        mine = mine + part
    mine = all_sum(mine, "space") / (total_loads * total_points)
    other = swap(mine, "param", 1)
    gram_time = jnp.where(
        half == 0,
        jnp.concatenate([mine, other]),
        jnp.concatenate([other, mine]),
    )

    core = jnp.zeros((own_rank, loads, points), jnp.float32)
    for i, chunk in enumerate(chunks):
        parts = [cores[i][:own_rank]]
        parts += [swap(pieces[i][k - 1], "tm", k) for k in range(1, n)]
        for k, part in enumerate(parts):
            j = me ^ k
            if chunk[0] == "load":
                at = (0, j * cut, chunk[1] * LANES)
            else:
                at = (0, chunk[2] * group, (chunk[1] * n + j) * LANES)
            core = lax.dynamic_update_slice(core, part, at)

    def load_gram(v):
        far = swap(v, "param", 1)
        both = jnp.where(
            half == 0,
            jnp.concatenate([v, far], axis=1),
            jnp.concatenate([far, v], axis=1),
        )
        return jnp.einsum("rps,rqs->pq", v, both, precision=precise_mode)

    param_part = jnp.zeros((loads, total_loads), jnp.float32)
    if mains * n < tiles:
        param_part = param_part + load_gram(core[:, :, mains * n * LANES :])
    for m in range(mains):
        tile = [c for c, chunk in zip(cores, chunks) if chunk[:2] == ("tile", m)]
        param_part = param_part + load_gram(jnp.concatenate(tile, axis=1))
    param_part = all_sum(all_sum_direct(param_part, "tm"), "space")
    gram_param = param_part / (rank * total_points)
    return (gram_time, core, gram_param)


def solution(mesh):
    placed = (P("tm", "param", "space"), P())
    return jax.shard_map(
        body,
        mesh=mesh,
        in_specs=placed,
        out_specs=(P("tm", None), P("tm", "param", "space"), P("param", None)),
        check_vma=False,
    )
```

```python
import functools

import jax
import jax.numpy as jnp
from jax import lax
from jax.experimental import pallas as pl
from jax.experimental.pallas import tpu as pltpu
from jax.sharding import PartitionSpec as P

LANES = 128
precise_mode = lax.Precision.HIGHEST


def xor_pairs(k, n):
    return [(i, i ^ k) for i in range(n)]


def swap(v, axis, k):
    return lax.ppermute(v, axis, xor_pairs(k, lax.axis_size(axis)))


def all_sum(v, axis):
    k = 1
    while k < lax.axis_size(axis):
        v = v + swap(v, axis, k)
        k *= 2
    return v


def split(v):
    high = v.astype(jnp.bfloat16)
    return high, (v - high.astype(jnp.float32)).astype(jnp.bfloat16)


def dot_t(a, b):
    return lax.dot_general(
        a, b, (((1,), (1,)), ((), ())), preferred_element_type=jnp.float32
    )


def pack_kernel(shifts, corner, snapshots, *refs):
    count = len(shifts)
    packed, (taken, taken_sem) = refs[:count], refs[count:]
    width = taken.shape[2]
    me = lax.axis_index("tm")
    loads = []
    for i, k in enumerate(shifts):
        load, lane = corner(me ^ k)
        source = snapshots.at[
            :,
            pl.ds(pl.multiple_of(load, 8), width),
            pl.ds(pl.multiple_of(lane, LANES), LANES),
        ]
        loads.append(pltpu.make_async_copy(source, taken.at[i], taken_sem.at[i]))
        loads[-1].start()
    for i in range(count):
        loads[i].wait()
        for p in range(width):
            packed[i][p] = taken[i, :, p, :]


def pack(snapshots, shifts, corner, width):
    rows = snapshots.shape[0]
    count = len(shifts)
    f32 = jnp.float32
    return pl.pallas_call(
        functools.partial(pack_kernel, shifts, corner),
        out_shape=[jax.ShapeDtypeStruct((width, rows, LANES), f32)] * count,
        in_specs=[pl.BlockSpec(memory_space=pl.ANY)],
        out_specs=[pl.BlockSpec(memory_space=pltpu.VMEM)] * count,
        scratch_shapes=[
            pltpu.VMEM((count, rows, width, LANES), f32),
            pltpu.SemaphoreType.DMA((count,)),
        ],
        compiler_params=pltpu.CompilerParams(vmem_limit_bytes=53 * 2**20),
        cost_estimate=pl.CostEstimate(
            flops=0, bytes_accessed=8 * count * width * rows * LANES, transcendentals=0
        ),
    )(snapshots)


def chunk_kernel(n, first, last, basis, *refs):
    blocks, refs = refs[:n], refs[n:]
    if not first:
        before, refs = refs[0], refs[1:]
    core, pieces, refs = refs[0], refs[1 : n + 1], refs[n + 1 :]
    if last:
        keep, send, total, high, low = refs
    else:
        total, high, low = refs
    me, half = lax.axis_index("tm"), lax.axis_index("param")
    loads, rows = blocks[0].shape[:2]
    rank = core.shape[0]
    for k in range(n):
        at = pl.ds(pl.multiple_of((me ^ k) * rows, rows), rows)
        for p in range(loads):
            h, l = split(blocks[k][p])
            high[at, p * LANES : (p + 1) * LANES] = h
            low[at, p * LANES : (p + 1) * LANES] = l
    h, l = high[...], low[...]
    product = dot_t(
        jnp.concatenate([h, h, l], axis=1), jnp.concatenate([h, l, h], axis=1)
    )
    if first:
        total[...] = product
    else:
        total[...] = before[...] + product
    if last:
        cut = keep.shape[1]
        for j in range(n):
            mine = pl.multiple_of(j * rows + half * cut, cut)
            other = pl.multiple_of(j * rows + (1 - half) * cut, cut)
            keep[j] = total[pl.ds(mine, cut), :]
            send[j] = total[pl.ds(other, cut), :]
    b = jnp.concatenate(split(basis[...]), axis=0)
    wide = jnp.dot(b, h, preferred_element_type=jnp.float32)
    wide = wide + jnp.dot(b, l, preferred_element_type=jnp.float32)
    values = wide[:rank] + wide[rank:]
    own = rank // n
    for p in range(loads):
        part = values[:, p * LANES : (p + 1) * LANES]
        core[:, p, :] = part
        for k in range(n):
            pieces[k][:, p, :] = part[k * own : (k + 1) * own]


def run_chunk(basis, blocks, before, last):
    n = len(blocks)
    loads, rows, lanes = blocks[0].shape
    steps = n * rows
    rank = basis.shape[0]
    first = before is None
    args = [basis, *blocks] + ([] if first else [before])
    f32 = lambda *dims: jax.ShapeDtypeStruct(dims, jnp.float32)
    shapes = [f32(rank, loads, lanes)] + [f32(rank // n, loads, lanes)] * n
    scratch = [pltpu.VMEM((steps, loads * lanes), jnp.bfloat16)] * 2
    if last:
        shapes += [f32(n, rows // 2, steps)] * 2
        scratch = [pltpu.VMEM((steps, steps), jnp.float32)] + scratch
    else:
        shapes += [f32(steps, steps)]
    points = loads * lanes
    return pl.pallas_call(
        functools.partial(chunk_kernel, n, first, last),
        out_shape=shapes,
        scratch_shapes=scratch,
        compiler_params=pltpu.CompilerParams(vmem_limit_bytes=40 * 2**20),
        cost_estimate=pl.CostEstimate(
            flops=2 * steps * points * (3 * steps + 4 * rank),
            bytes_accessed=4 * steps * (points + 2 * steps),
            transcendentals=0,
        ),
    )(*args)


def load_products(left, right):
    rank = left[0].shape[0]
    many = 16 if rank % 16 == 0 else rank

    def tiles(refs, first):
        rows = [
            jnp.concatenate([ref[r] for ref in refs])
            for r in range(first, first + many)
        ]
        return jnp.concatenate(split(jnp.concatenate(rows, axis=1)), axis=0)

    acc = 0.0
    for r in range(0, rank, many):
        acc = acc + dot_t(tiles(left, r), tiles(right, r))
    rows, columns = acc.shape[0] // 2, acc.shape[1] // 2
    acc = acc[:rows] + acc[rows:]
    return acc[:, :columns] + acc[:, columns:]


def load_gram_kernel(groups, *refs):
    own, far, out = refs[:groups], refs[groups:-1], refs[-1]
    out[...] = load_products(own, own + far)


def load_gram(own, far):
    loads = sum(v.shape[1] for v in own)
    both = loads + sum(v.shape[1] for v in far)
    return pl.pallas_call(
        functools.partial(load_gram_kernel, len(own)),
        out_shape=jax.ShapeDtypeStruct((loads, both), jnp.float32),
    )(*own, *far)


def fold_kernel(n, groups, keep, got, far, part, rest, *refs):
    own, outs = refs[:groups], refs[groups:]
    me, half = lax.axis_index("tm"), lax.axis_index("param")
    loads = part.shape[0]
    total = jnp.concatenate([part[...], load_products(own, [far])], axis=1)
    swapped = jnp.concatenate([total[:, loads:], total[:, :loads]], axis=1)
    total = jnp.where(half == 0, total, swapped) + rest[...]
    total = jnp.concatenate(
        [total, jnp.zeros((loads, LANES - 2 * loads), jnp.float32)], axis=1
    )
    cut = keep.shape[1]
    for k in range(n):
        outs[k][:cut] = keep[me ^ k] + got[me ^ k]
        for b in range(loads // 8):
            outs[k][cut:, b * LANES : (b + 1) * LANES] = total[b * 8 : (b + 1) * 8]


def fold(keep, got, far, part, rest, own):
    n, cut, steps = keep.shape
    shape = jax.ShapeDtypeStruct((cut + 8, steps), jnp.float32)
    return pl.pallas_call(
        functools.partial(fold_kernel, n, len(own)),
        out_shape=[shape] * n,
    )(keep, got, far, part, rest, *own)


def place_kernel(n, places, *refs):
    out = refs[-1]
    me = lax.axis_index("tm")
    for where, piece in zip(places, refs):
        load, lane = where(me)
        count = piece.shape[1]
        at = pl.ds(pl.multiple_of(load, 8), count)
        out[:, at, pl.ds(pl.multiple_of(lane, LANES), LANES)] = piece[...]


def place_pieces(n, places, pieces, shape):
    specs = []
    for piece in pieces:
        block = (shape[0],) + piece.shape[1:]
        specs.append(pl.BlockSpec(block, lambda i: (0, 0, 0)))
    return pl.pallas_call(
        functools.partial(place_kernel, n, places),
        out_shape=jax.ShapeDtypeStruct(shape, jnp.float32),
        grid=(1,),
        in_specs=specs,
        out_specs=pl.BlockSpec(shape, lambda i: (0, 0, 0)),
        compiler_params=pltpu.CompilerParams(vmem_limit_bytes=16 * 2**20),
    )(*pieces)


def after(v, *others):
    return lax.optimization_barrier((v, others))[0]


def body(snapshots, time_basis):
    rows, loads, points = snapshots.shape
    n = lax.axis_size("tm")
    me, half = lax.axis_index("tm"), lax.axis_index("param")
    rank = time_basis.shape[1]
    own_rank = rank // n
    total_points = points * lax.axis_size("space")
    total_loads = loads * lax.axis_size("param")
    tiles = points // LANES
    cut = loads // n
    mains = tiles // n
    group = 8 if loads % 8 == 0 else loads
    groups = loads // group
    others = tuple(range(1, n))

    chunks = [("load", t) for t in range(mains * n, tiles)]
    chunks += [("tile", m, g) for m in range(mains) for g in range(groups)]
    n_load = tiles - mains * n

    order = me ^ jnp.arange(n)
    basis = time_basis.reshape(-1, n, own_rank)[:, order].reshape(-1, rank).T

    def corner(chunk, j):
        if chunk[0] == "load":
            return j * cut, chunk[1] * LANES
        return chunk[2] * group, (chunk[1] * n + j) * LANES

    def shares(x, chunk, shifts):
        width = cut if chunk[0] == "load" else group
        if width % 8 == 0:
            return pack(x, shifts, functools.partial(corner, chunk), width)
        out = []
        for k in shifts:
            load, lane = corner(chunk, me ^ k)
            v = lax.dynamic_slice(x, (0, load, lane), (rows, width, LANES))
            out.append(v.transpose(1, 0, 2))
        return out

    sent = []

    def send(v, k, depth=4):
        if len(sent) >= depth:
            v = after(v, sent[-depth])
        sent.append(swap(v, "tm", k))
        return sent[-1]

    pick = lambda v, k: lax.dynamic_index_in_dim(v, me ^ k, 0, False)
    place_of = lambda i, k: lambda me: corner(chunks[i], me ^ k)
    held, cores, pieces, far = [], [], [], []
    places, placed = [], []
    total = param_part = None

    def send_pieces(first, last, depth=4):
        for k in others:
            parts = [pieces[i][k] for i in range(first, last)]
            part = parts[0] if len(parts) == 1 else jnp.concatenate(parts, axis=1)
            part = send(part, k, depth)
            if chunks[first][0] == "load":
                width = part.shape[1] // (last - first)
                for i in range(first, last):
                    places.append(place_of(i, k))
                    placed.append(part[:, (i - first) * width : (i - first + 1) * width])
            else:
                places.append(place_of(first, k))
                placed.append(part)

    def chunk_done(i):
        nonlocal total
        x = after(snapshots, held[i - 1][0]) if i else snapshots
        own = shares(x, chunks[i], (0,))[0]
        before, partners = total, held[i]
        last = i == len(chunks) - 1
        if last and i:
            before, partners = after((before, partners), param_part, far)
        out = run_chunk(basis, [own, *partners], before, last)
        cores.append(out[0])
        pieces.append(out[1 : n + 1])
        total = out[n + 1 :] if last else out[n + 1]
        if chunks[i][0] == "tile" and not last:
            far.append(swap(cores[i], "param", 1))
        for_own = pieces[i][0]
        places.append(place_of(i, 0))
        placed.append(for_own)

    def put(core, part, at):
        return lax.dynamic_update_slice(core, part, at)

    def load_part():
        rest = []
        for i in range(n_load):
            tile = jnp.zeros((own_rank, loads, LANES), jnp.float32)
            for where, part in zip(places, placed):
                load, lane = where(me)
                if where(0)[1] == chunks[i][1] * LANES:
                    tile = put(tile, part, (0, load, 0))
            rest.append(tile)
        rest = jnp.concatenate(rest, axis=2)
        other = swap(rest, "param", 1)
        both = jnp.where(
            half == 0,
            jnp.concatenate([rest, other], axis=1),
            jnp.concatenate([other, rest], axis=1),
        )
        return jnp.einsum("rps,rqs->pq", rest, both, precision=precise_mode)

    ahead = 2
    load_sent = n_load == 0
    packs = ()
    for i, chunk in enumerate(chunks):
        x = after(snapshots, packs, held[i - 3] if i >= 3 else ())
        packs = parts = shares(x, chunk, others)
        held.append([send(v, k) for v, k in zip(parts, others)])
        if i >= ahead:
            chunk_done(i - ahead)
        if len(cores) == n_load and not load_sent and mains:
            send_pieces(0, n_load)
            load_sent = True
            param_part = load_part()
    for i in range(len(chunks) - ahead, len(chunks)):
        chunk_done(i)
    if not load_sent:
        send_pieces(0, n_load)
        param_part = load_part()
    keep, other_half = total
    wide = -(-total_loads // LANES) * LANES
    steps = n * rows
    across = steps // wide
    fused = mains == 1 and group == 8 and loads * LANES == 8 * steps and n_load
    got = swap(other_half, "param", 1)
    if fused:
        far_last = swap(cores[-1], "param", 1)
        part = load_gram(cores[n_load:], far)
        mixed = fold(keep, got, far_last, part, param_part, cores[n_load:])
    else:
        if mains:
            far.append(swap(cores[-1], "param", 1))
        for m in range(mains):
            these = slice(m * groups, (m + 1) * groups)
            part = load_gram(cores[n_load:][these], far[these])
            swapped = jnp.concatenate([part[:, loads:], part[:, :loads]], axis=1)
            part = jnp.where(half == 0, part, swapped)
            param_part = part if param_part is None else param_part + part
        padded = jnp.pad(param_part, ((0, 0), (0, wide - total_loads)))
        extra = padded.reshape(across, loads // across, wide).swapaxes(0, 1)
        extra = extra.reshape(loads // across, steps)
        rows_part = keep + got
        mixed = [jnp.concatenate([pick(rows_part, k), extra]) for k in range(n)]
    arrived = [send(mixed[k], k) for k in others]
    mine = mixed[0]
    for part in arrived:
        mine = mine + part
    mine = all_sum(mine, "space")

    for m in range(mains):
        at = n_load + m * groups
        send_pieces(at, at + groups)
    if cut % 8 == 0 and group % 8 == 0:
        core = place_pieces(n, places, placed, (own_rank, loads, points))
    else:
        core = jnp.zeros((own_rank, loads, points), jnp.float32)
        for where, part in zip(places, placed):
            core = put(core, part, (0, *where(me)))

    extra = mine[rows // 2 :].reshape(loads // across, across, wide).swapaxes(0, 1)
    gram_param = extra.reshape(loads, wide)[:, :total_loads] / (rank * total_points)
    other = swap(mine, "param", 1)[: rows // 2]
    mine = mine[: rows // 2]
    gram_time = jnp.where(
        half == 0,
        jnp.concatenate([mine, other]),
        jnp.concatenate([other, mine]),
    )
    gram_time = gram_time / (total_loads * total_points)
    return (gram_time, core, gram_param)


def solution(mesh):
    placed = (P("tm", "param", "space"), P())
    return jax.shard_map(
        body,
        mesh=mesh,
        in_specs=placed,
        out_specs=(P("tm", None), P("tm", "param", "space"), P("param", None)),
        check_vma=False,
    )
```

```python
import functools

import jax
import jax.numpy as jnp
from jax import lax
from jax.experimental import pallas as pl
from jax.experimental.pallas import tpu as pltpu
from jax.sharding import PartitionSpec as P

LANES = 128
precise_mode = lax.Precision.HIGHEST


def xor_pairs(k, n):
    return [(i, i ^ k) for i in range(n)]


def swap(v, axis, k):
    return lax.ppermute(v, axis, xor_pairs(k, lax.axis_size(axis)))


def all_sum(v, axis):
    k = 1
    while k < lax.axis_size(axis):
        v = v + swap(v, axis, k)
        k *= 2
    return v


def split(v):
    high = v.astype(jnp.bfloat16)
    return high, (v - high.astype(jnp.float32)).astype(jnp.bfloat16)


def dot_t(a, b):
    return lax.dot_general(
        a, b, (((1,), (1,)), ((), ())), preferred_element_type=jnp.float32
    )


def pack_kernel(shifts, corner, snapshots, *refs):
    count = len(shifts)
    packed, (taken, taken_sem) = refs[:count], refs[count:]
    width = taken.shape[2]
    me = lax.axis_index("tm")
    loads = []
    for i, k in enumerate(shifts):
        load, lane = corner(me ^ k)
        source = snapshots.at[
            :,
            pl.ds(pl.multiple_of(load, 8), width),
            pl.ds(pl.multiple_of(lane, LANES), LANES),
        ]
        loads.append(pltpu.make_async_copy(source, taken.at[i], taken_sem.at[i]))
        loads[-1].start()
    for i in range(count):
        loads[i].wait()
        for p in range(width):
            packed[i][p] = taken[i, :, p, :]


def pack(snapshots, shifts, corner, width):
    rows = snapshots.shape[0]
    count = len(shifts)
    f32 = jnp.float32
    return pl.pallas_call(
        functools.partial(pack_kernel, shifts, corner),
        out_shape=[jax.ShapeDtypeStruct((width, rows, LANES), f32)] * count,
        in_specs=[pl.BlockSpec(memory_space=pl.ANY)],
        out_specs=[pl.BlockSpec(memory_space=pltpu.VMEM)] * count,
        scratch_shapes=[
            pltpu.VMEM((count, rows, width, LANES), f32),
            pltpu.SemaphoreType.DMA((count,)),
        ],
        compiler_params=pltpu.CompilerParams(vmem_limit_bytes=53 * 2**20),
        cost_estimate=pl.CostEstimate(
            flops=0, bytes_accessed=8 * count * width * rows * LANES, transcendentals=0
        ),
    )(snapshots)


def chunk_kernel(n, first, last, basis, *refs):
    blocks, refs = refs[:n], refs[n:]
    if not first:
        before, refs = refs[0], refs[1:]
    core, pieces, refs = refs[0], refs[1 : n + 1], refs[n + 1 :]
    if last:
        keep, send, total, high, low = refs
    else:
        total, high, low = refs
    me, half = lax.axis_index("tm"), lax.axis_index("param")
    loads, rows = blocks[0].shape[:2]
    rank = core.shape[0]
    for k in range(n):
        at = pl.ds(pl.multiple_of((me ^ k) * rows, rows), rows)
        for p in range(loads):
            h, l = split(blocks[k][p])
            high[at, p * LANES : (p + 1) * LANES] = h
            low[at, p * LANES : (p + 1) * LANES] = l
    h, l = high[...], low[...]
    product = dot_t(
        jnp.concatenate([h, h, l], axis=1), jnp.concatenate([h, l, h], axis=1)
    )
    if first:
        total[...] = product
    else:
        total[...] = before[...] + product
    if last:
        cut = keep.shape[1]
        for j in range(n):
            mine = pl.multiple_of(j * rows + half * cut, cut)
            other = pl.multiple_of(j * rows + (1 - half) * cut, cut)
            keep[j] = total[pl.ds(mine, cut), :]
            send[j] = total[pl.ds(other, cut), :]
    b = jnp.concatenate(split(basis[...]), axis=0)
    wide = jnp.dot(b, h, preferred_element_type=jnp.float32)
    wide = wide + jnp.dot(b, l, preferred_element_type=jnp.float32)
    values = wide[:rank] + wide[rank:]
    own = rank // n
    for p in range(loads):
        part = values[:, p * LANES : (p + 1) * LANES]
        core[:, p, :] = part
        for k in range(n):
            pieces[k][:, p, :] = part[k * own : (k + 1) * own]


def run_chunk(basis, blocks, before, last):
    n = len(blocks)
    loads, rows, lanes = blocks[0].shape
    steps = n * rows
    rank = basis.shape[0]
    first = before is None
    args = [basis, *blocks] + ([] if first else [before])
    f32 = lambda *dims: jax.ShapeDtypeStruct(dims, jnp.float32)
    shapes = [f32(rank, loads, lanes)] + [f32(rank // n, loads, lanes)] * n
    scratch = [pltpu.VMEM((steps, loads * lanes), jnp.bfloat16)] * 2
    if last:
        shapes += [f32(n, rows // 2, steps)] * 2
        scratch = [pltpu.VMEM((steps, steps), jnp.float32)] + scratch
    else:
        shapes += [f32(steps, steps)]
    points = loads * lanes
    return pl.pallas_call(
        functools.partial(chunk_kernel, n, first, last),
        out_shape=shapes,
        scratch_shapes=scratch,
        compiler_params=pltpu.CompilerParams(vmem_limit_bytes=24 * 2**20),
        cost_estimate=pl.CostEstimate(
            flops=2 * steps * points * (3 * steps + 4 * rank),
            bytes_accessed=4 * steps * (points + 2 * steps),
            transcendentals=0,
        ),
    )(*args)


def load_products(left, right):
    rank = left[0].shape[0]
    many = 16 if rank % 16 == 0 else rank

    def tiles(refs, first):
        rows = [
            jnp.concatenate([ref[r] for ref in refs])
            for r in range(first, first + many)
        ]
        return jnp.concatenate(split(jnp.concatenate(rows, axis=1)), axis=0)

    acc = 0.0
    for r in range(0, rank, many):
        acc = acc + dot_t(tiles(left, r), tiles(right, r))
    rows, columns = acc.shape[0] // 2, acc.shape[1] // 2
    acc = acc[:rows] + acc[rows:]
    return acc[:, :columns] + acc[:, columns:]


def load_gram_kernel(groups, *refs):
    own, far, out = refs[:groups], refs[groups:-1], refs[-1]
    out[...] = load_products(own, own + far)


def load_gram(own, far):
    loads = sum(v.shape[1] for v in own)
    both = loads + sum(v.shape[1] for v in far)
    return pl.pallas_call(
        functools.partial(load_gram_kernel, len(own)),
        out_shape=jax.ShapeDtypeStruct((loads, both), jnp.float32),
        compiler_params=pltpu.CompilerParams(vmem_limit_bytes=12 * 2**20),
    )(*own, *far)


def fold_kernel(n, groups, keep, got, far, part, rest, *refs):
    own, outs = refs[:groups], refs[groups:]
    me, half = lax.axis_index("tm"), lax.axis_index("param")
    loads = part.shape[0]
    total = jnp.concatenate([part[...], load_products(own, [far])], axis=1)
    swapped = jnp.concatenate([total[:, loads:], total[:, :loads]], axis=1)
    total = jnp.where(half == 0, total, swapped) + rest[...]
    total = jnp.concatenate(
        [total, jnp.zeros((loads, LANES - 2 * loads), jnp.float32)], axis=1
    )
    cut = keep.shape[1]
    for k in range(n):
        outs[k][:cut] = keep[me ^ k] + got[me ^ k]
        for b in range(loads // 8):
            outs[k][cut:, b * LANES : (b + 1) * LANES] = total[b * 8 : (b + 1) * 8]


def fold(keep, got, far, part, rest, own):
    n, cut, steps = keep.shape
    shape = jax.ShapeDtypeStruct((cut + 8, steps), jnp.float32)
    return pl.pallas_call(
        functools.partial(fold_kernel, n, len(own)),
        out_shape=[shape] * n,
        compiler_params=pltpu.CompilerParams(vmem_limit_bytes=12 * 2**20),
    )(keep, got, far, part, rest, *own)


def place_kernel(n, places, *refs):
    out = refs[-1]
    me = lax.axis_index("tm")
    for where, piece in zip(places, refs):
        load, lane = where(me)
        count = piece.shape[1]
        at = pl.ds(pl.multiple_of(load, 8), count)
        out[:, at, pl.ds(pl.multiple_of(lane, LANES), LANES)] = piece[...]


def place_pieces(n, places, pieces, shape):
    specs = []
    for piece in pieces:
        block = (shape[0],) + piece.shape[1:]
        specs.append(pl.BlockSpec(block, lambda i: (0, 0, 0)))
    return pl.pallas_call(
        functools.partial(place_kernel, n, places),
        out_shape=jax.ShapeDtypeStruct(shape, jnp.float32),
        grid=(1,),
        in_specs=specs,
        out_specs=pl.BlockSpec(shape, lambda i: (0, 0, 0)),
        compiler_params=pltpu.CompilerParams(vmem_limit_bytes=8 * 2**20),
    )(*pieces)


def after(v, *others):
    return lax.optimization_barrier((v, others))[0]


def body(snapshots, time_basis):
    rows, loads, points = snapshots.shape
    n = lax.axis_size("tm")
    me, half = lax.axis_index("tm"), lax.axis_index("param")
    rank = time_basis.shape[1]
    own_rank = rank // n
    total_points = points * lax.axis_size("space")
    total_loads = loads * lax.axis_size("param")
    tiles = points // LANES
    cut = loads // n
    mains = tiles // n
    group = 8 if loads % 8 == 0 else loads
    groups = loads // group
    others = tuple(range(1, n))

    chunks = [("load", t) for t in range(mains * n, tiles)]
    chunks += [("tile", m, g) for m in range(mains) for g in range(groups)]
    n_load = tiles - mains * n

    order = me ^ jnp.arange(n)
    basis = time_basis.reshape(-1, n, own_rank)[:, order].reshape(-1, rank).T

    def corner(chunk, j):
        if chunk[0] == "load":
            return j * cut, chunk[1] * LANES
        return chunk[2] * group, (chunk[1] * n + j) * LANES

    def shares(x, chunk, shifts):
        width = cut if chunk[0] == "load" else group
        if width % 8 == 0:
            return pack(x, shifts, functools.partial(corner, chunk), width)
        out = []
        for k in shifts:
            load, lane = corner(chunk, me ^ k)
            v = lax.dynamic_slice(x, (0, load, lane), (rows, width, LANES))
            out.append(v.transpose(1, 0, 2))
        return out

    sent = []

    def send(v, k, depth=4):
        if len(sent) >= depth:
            v = after(v, sent[-depth])
        sent.append(swap(v, "tm", k))
        return sent[-1]

    pick = lambda v, k: lax.dynamic_index_in_dim(v, me ^ k, 0, False)
    place_of = lambda i, k: lambda me: corner(chunks[i], me ^ k)
    held, cores, pieces, far = [], [], [], []
    places, placed = [], []
    total = param_part = None

    def send_pieces(first, last, depth=4):
        for k in others:
            parts = [pieces[i][k] for i in range(first, last)]
            part = parts[0] if len(parts) == 1 else jnp.concatenate(parts, axis=1)
            part = send(part, k, depth)
            if chunks[first][0] == "load":
                width = part.shape[1] // (last - first)
                for i in range(first, last):
                    places.append(place_of(i, k))
                    placed.append(part[:, (i - first) * width : (i - first + 1) * width])
            else:
                places.append(place_of(first, k))
                placed.append(part)

    def chunk_done(i):
        nonlocal total
        x = after(snapshots, held[i - 1][0]) if i else snapshots
        own = shares(x, chunks[i], (0,))[0]
        before, partners = total, held[i]
        last = i == len(chunks) - 1
        if last and i:
            before, partners = after((before, partners), param_part, far)
        out = run_chunk(basis, [own, *partners], before, last)
        cores.append(out[0])
        pieces.append(out[1 : n + 1])
        total = out[n + 1 :] if last else out[n + 1]
        if chunks[i][0] == "tile" and not last:
            far.append(swap(cores[i], "param", 1))
        for_own = pieces[i][0]
        places.append(place_of(i, 0))
        placed.append(for_own)

    def put(core, part, at):
        return lax.dynamic_update_slice(core, part, at)

    def load_part():
        rest = []
        for i in range(n_load):
            tile = jnp.zeros((own_rank, loads, LANES), jnp.float32)
            for where, part in zip(places, placed):
                load, lane = where(me)
                if where(0)[1] == chunks[i][1] * LANES:
                    tile = put(tile, part, (0, load, 0))
            rest.append(tile)
        rest = jnp.concatenate(rest, axis=2)
        other = swap(rest, "param", 1)
        both = jnp.where(
            half == 0,
            jnp.concatenate([rest, other], axis=1),
            jnp.concatenate([other, rest], axis=1),
        )
        return jnp.einsum("rps,rqs->pq", rest, both, precision=precise_mode)

    ahead = 2
    load_sent = n_load == 0
    packs = ()
    for i, chunk in enumerate(chunks):
        x = after(snapshots, packs, held[i - 3] if i >= 3 else ())
        packs = parts = shares(x, chunk, others)
        held.append([send(v, k) for v, k in zip(parts, others)])
        if i >= ahead:
            chunk_done(i - ahead)
        if len(cores) == n_load and not load_sent and mains:
            send_pieces(0, n_load)
            load_sent = True
            param_part = load_part()
    for i in range(len(chunks) - ahead, len(chunks)):
        chunk_done(i)
    if not load_sent:
        send_pieces(0, n_load)
        param_part = load_part()
    keep, other_half = total
    wide = -(-total_loads // LANES) * LANES
    steps = n * rows
    across = steps // wide
    fused = mains == 1 and group == 8 and loads * LANES == 8 * steps and n_load
    got = swap(other_half, "param", 1)
    if fused:
        far_last = swap(cores[-1], "param", 1)
        part = load_gram(cores[n_load:], far)
        mixed = fold(keep, got, far_last, part, param_part, cores[n_load:])
    else:
        if mains:
            far.append(swap(cores[-1], "param", 1))
        for m in range(mains):
            these = slice(m * groups, (m + 1) * groups)
            part = load_gram(cores[n_load:][these], far[these])
            swapped = jnp.concatenate([part[:, loads:], part[:, :loads]], axis=1)
            part = jnp.where(half == 0, part, swapped)
            param_part = part if param_part is None else param_part + part
        padded = jnp.pad(param_part, ((0, 0), (0, wide - total_loads)))
        extra = padded.reshape(across, loads // across, wide).swapaxes(0, 1)
        extra = extra.reshape(loads // across, steps)
        rows_part = keep + got
        mixed = [jnp.concatenate([pick(rows_part, k), extra]) for k in range(n)]
    arrived = [send(mixed[k], k) for k in others]
    mine = mixed[0]
    for part in arrived:
        mine = mine + part
    mine = all_sum(mine, "space")

    for m in range(mains):
        at = n_load + m * groups
        send_pieces(at, at + groups)
    if cut % 8 == 0 and group % 8 == 0:
        core = place_pieces(n, places, placed, (own_rank, loads, points))
    else:
        core = jnp.zeros((own_rank, loads, points), jnp.float32)
        for where, part in zip(places, placed):
            core = put(core, part, (0, *where(me)))

    extra = mine[rows // 2 :].reshape(loads // across, across, wide).swapaxes(0, 1)
    gram_param = extra.reshape(loads, wide)[:, :total_loads] / (rank * total_points)
    other = swap(mine, "param", 1)[: rows // 2]
    mine = mine[: rows // 2]
    gram_time = jnp.where(
        half == 0,
        jnp.concatenate([mine, other]),
        jnp.concatenate([other, mine]),
    )
    gram_time = gram_time / (total_loads * total_points)
    return (gram_time, core, gram_param)


def solution(mesh):
    placed = (P("tm", "param", "space"), P())
    return jax.shard_map(
        body,
        mesh=mesh,
        in_specs=placed,
        out_specs=(P("tm", None), P("tm", "param", "space"), P("param", None)),
        check_vma=False,
    )
```

```python
import functools

import jax
import jax.numpy as jnp
from jax import lax
from jax.experimental import pallas as pl
from jax.experimental.pallas import tpu as pltpu
from jax.sharding import PartitionSpec as P

LANES = 128
precise_mode = lax.Precision.HIGHEST


def xor_pairs(k, n):
    return [(i, i ^ k) for i in range(n)]


def swap(v, axis, k):
    return lax.ppermute(v, axis, xor_pairs(k, lax.axis_size(axis)))


def all_sum(v, axis):
    k = 1
    while k < lax.axis_size(axis):
        v = v + swap(v, axis, k)
        k *= 2
    return v


def split(v):
    high = v.astype(jnp.bfloat16)
    return high, (v - high.astype(jnp.float32)).astype(jnp.bfloat16)


def dot_t(a, b):
    return lax.dot_general(
        a, b, (((1,), (1,)), ((), ())), preferred_element_type=jnp.float32
    )


def pack_kernel(shifts, corner, width, turn, snapshots, *refs):
    count = len(shifts)
    packed, (*taken, taken_sem) = refs[:count], refs[count:]
    me = lax.axis_index("tm")
    loads = []
    for i, k in enumerate(shifts):
        load, lane = corner(me ^ k)
        source = snapshots.at[
            :,
            pl.ds(pl.multiple_of(load, 8), width),
            pl.ds(pl.multiple_of(lane, LANES), LANES),
        ]
        target = taken[0].at[i] if turn else packed[i]
        loads.append(pltpu.make_async_copy(source, target, taken_sem.at[i]))
        loads[-1].start()
    for i in range(count):
        loads[i].wait()
        if turn:
            for p in range(width):
                packed[i][p] = taken[0][i, :, p, :]


def pack(snapshots, shifts, corner, width, turn):
    rows = snapshots.shape[0]
    count = len(shifts)
    f32 = jnp.float32
    shape = (width, rows, LANES) if turn else (rows, width, LANES)
    scratch = [pltpu.VMEM((count, rows, width, LANES), f32)] if turn else []
    return pl.pallas_call(
        functools.partial(pack_kernel, shifts, corner, width, turn),
        out_shape=[jax.ShapeDtypeStruct(shape, f32)] * count,
        in_specs=[pl.BlockSpec(memory_space=pl.ANY)],
        out_specs=[pl.BlockSpec(memory_space=pltpu.VMEM)] * count,
        scratch_shapes=scratch + [pltpu.SemaphoreType.DMA((count,))],
        compiler_params=pltpu.CompilerParams(vmem_limit_bytes=53 * 2**20),
        cost_estimate=pl.CostEstimate(
            flops=0, bytes_accessed=8 * count * width * rows * LANES, transcendentals=0
        ),
    )(snapshots)


def chunk_kernel(n, first, last, basis, *refs):
    blocks, refs = refs[:n], refs[n:]
    if not first:
        before, refs = refs[0], refs[1:]
    core, pieces, refs = refs[0], refs[1 : n + 1], refs[n + 1 :]
    if last:
        keep, send, total, high, low, turned = refs
    else:
        total, high, low, turned = refs
    me, half = lax.axis_index("tm"), lax.axis_index("param")
    loads, rows = blocks[0].shape[:2]
    rank = core.shape[0]
    for k in range(n):
        at = pl.ds(pl.multiple_of((me ^ k) * rows, rows), rows)
        block = blocks[k]
        if block.shape[0] != loads:
            block = turned
            for p in range(loads):
                turned[p] = blocks[k][:, p, :]
        for p in range(loads):
            h, l = split(block[p])
            high[at, p * LANES : (p + 1) * LANES] = h
            low[at, p * LANES : (p + 1) * LANES] = l
    h, l = high[...], low[...]
    product = dot_t(
        jnp.concatenate([h, h, l], axis=1), jnp.concatenate([h, l, h], axis=1)
    )
    if first:
        total[...] = product
    else:
        total[...] = before[...] + product
    if last:
        cut = keep.shape[1]
        for j in range(n):
            mine = pl.multiple_of(j * rows + half * cut, cut)
            other = pl.multiple_of(j * rows + (1 - half) * cut, cut)
            keep[j] = total[pl.ds(mine, cut), :]
            send[j] = total[pl.ds(other, cut), :]
    b = jnp.concatenate(split(basis[...]), axis=0)
    wide = jnp.dot(b, h, preferred_element_type=jnp.float32)
    wide = wide + jnp.dot(b, l, preferred_element_type=jnp.float32)
    values = wide[:rank] + wide[rank:]
    own = rank // n
    for p in range(loads):
        part = values[:, p * LANES : (p + 1) * LANES]
        core[:, p, :] = part
        for k in range(n):
            pieces[k][:, p, :] = part[k * own : (k + 1) * own]


def run_chunk(basis, blocks, before, last):
    n = len(blocks)
    loads, rows, lanes = blocks[0].shape
    steps = n * rows
    rank = basis.shape[0]
    first = before is None
    args = [basis, *blocks] + ([] if first else [before])
    f32 = lambda *dims: jax.ShapeDtypeStruct(dims, jnp.float32)
    shapes = [f32(rank, loads, lanes)] + [f32(rank // n, loads, lanes)] * n
    scratch = [pltpu.VMEM((steps, loads * lanes), jnp.bfloat16)] * 2
    scratch.append(pltpu.VMEM((loads, rows, lanes), jnp.float32))
    if last:
        shapes += [f32(n, rows // 2, steps)] * 2
        scratch = [pltpu.VMEM((steps, steps), jnp.float32)] + scratch
    else:
        shapes += [f32(steps, steps)]
    points = loads * lanes
    return pl.pallas_call(
        functools.partial(chunk_kernel, n, first, last),
        out_shape=shapes,
        scratch_shapes=scratch,
        compiler_params=pltpu.CompilerParams(vmem_limit_bytes=24 * 2**20),
        cost_estimate=pl.CostEstimate(
            flops=2 * steps * points * (3 * steps + 4 * rank),
            bytes_accessed=4 * steps * (points + 2 * steps),
            transcendentals=0,
        ),
    )(*args)


def load_products(left, right):
    rank = left[0].shape[0]
    many = 16 if rank % 16 == 0 else rank

    def tiles(refs, first):
        rows = [
            jnp.concatenate([ref[r] for ref in refs])
            for r in range(first, first + many)
        ]
        return jnp.concatenate(split(jnp.concatenate(rows, axis=1)), axis=0)

    acc = 0.0
    for r in range(0, rank, many):
        acc = acc + dot_t(tiles(left, r), tiles(right, r))
    rows, columns = acc.shape[0] // 2, acc.shape[1] // 2
    acc = acc[:rows] + acc[rows:]
    return acc[:, :columns] + acc[:, columns:]


def load_gram_kernel(groups, *refs):
    own, far, out = refs[:groups], refs[groups:-1], refs[-1]
    out[...] = load_products(own, own + far)


def load_gram(own, far):
    loads = sum(v.shape[1] for v in own)
    both = loads + sum(v.shape[1] for v in far)
    return pl.pallas_call(
        functools.partial(load_gram_kernel, len(own)),
        out_shape=jax.ShapeDtypeStruct((loads, both), jnp.float32),
        compiler_params=pltpu.CompilerParams(vmem_limit_bytes=12 * 2**20),
    )(*own, *far)


def fold_kernel(n, groups, keep, got, far, part, rest, *refs):
    own, outs = refs[:groups], refs[groups:]
    me, half = lax.axis_index("tm"), lax.axis_index("param")
    loads = part.shape[0]
    total = jnp.concatenate([part[...], load_products(own, [far])], axis=1)
    swapped = jnp.concatenate([total[:, loads:], total[:, :loads]], axis=1)
    total = jnp.where(half == 0, total, swapped) + rest[...]
    total = jnp.concatenate(
        [total, jnp.zeros((loads, LANES - 2 * loads), jnp.float32)], axis=1
    )
    cut = keep.shape[1]
    for k in range(n):
        outs[k][:cut] = keep[me ^ k] + got[me ^ k]
        for b in range(loads // 8):
            outs[k][cut:, b * LANES : (b + 1) * LANES] = total[b * 8 : (b + 1) * 8]


def fold(keep, got, far, part, rest, own):
    n, cut, steps = keep.shape
    shape = jax.ShapeDtypeStruct((cut + 8, steps), jnp.float32)
    return pl.pallas_call(
        functools.partial(fold_kernel, n, len(own)),
        out_shape=[shape] * n,
        compiler_params=pltpu.CompilerParams(vmem_limit_bytes=12 * 2**20),
    )(keep, got, far, part, rest, *own)


def place_kernel(n, places, *refs):
    out = refs[-1]
    me = lax.axis_index("tm")
    for where, piece in zip(places, refs):
        load, lane = where(me)
        count = piece.shape[1]
        at = pl.ds(pl.multiple_of(load, 8), count)
        out[:, at, pl.ds(pl.multiple_of(lane, LANES), LANES)] = piece[...]


def place_pieces(n, places, pieces, shape):
    specs = []
    for piece in pieces:
        block = (shape[0],) + piece.shape[1:]
        specs.append(pl.BlockSpec(block, lambda i: (0, 0, 0)))
    return pl.pallas_call(
        functools.partial(place_kernel, n, places),
        out_shape=jax.ShapeDtypeStruct(shape, jnp.float32),
        grid=(1,),
        in_specs=specs,
        out_specs=pl.BlockSpec(shape, lambda i: (0, 0, 0)),
        compiler_params=pltpu.CompilerParams(vmem_limit_bytes=8 * 2**20),
    )(*pieces)


def after(v, *others):
    return lax.optimization_barrier((v, others))[0]


def body(snapshots, time_basis):
    rows, loads, points = snapshots.shape
    n = lax.axis_size("tm")
    me, half = lax.axis_index("tm"), lax.axis_index("param")
    rank = time_basis.shape[1]
    own_rank = rank // n
    total_points = points * lax.axis_size("space")
    total_loads = loads * lax.axis_size("param")
    tiles = points // LANES
    cut = loads // n
    mains = tiles // n
    group = 8 if loads % 8 == 0 else loads
    groups = loads // group
    others = tuple(range(1, n))

    chunks = [("load", t) for t in range(mains * n, tiles)]
    chunks += [("tile", m, g) for m in range(mains) for g in range(groups)]
    n_load = tiles - mains * n

    order = me ^ jnp.arange(n)
    basis = time_basis.reshape(-1, n, own_rank)[:, order].reshape(-1, rank).T

    def corner(chunk, j):
        if chunk[0] == "load":
            return j * cut, chunk[1] * LANES
        return chunk[2] * group, (chunk[1] * n + j) * LANES

    def shares(x, chunk, shifts):
        width = cut if chunk[0] == "load" else group
        if width % 8 == 0:
            turn = chunk != chunks[0] or shifts == (0,)
            return pack(x, shifts, functools.partial(corner, chunk), width, turn)
        out = []
        for k in shifts:
            load, lane = corner(chunk, me ^ k)
            v = lax.dynamic_slice(x, (0, load, lane), (rows, width, LANES))
            out.append(v.transpose(1, 0, 2))
        return out

    sent = []

    def send(v, k, depth=4):
        if len(sent) >= depth:
            v = after(v, sent[-depth])
        out = swap(v, "tm", k)
        if depth < 99:
            sent.append(out)
        return out

    pick = lambda v, k: lax.dynamic_index_in_dim(v, me ^ k, 0, False)
    place_of = lambda i, k: lambda me: corner(chunks[i], me ^ k)
    held, cores, pieces, far = [], [], [], []
    places, placed = [], []
    total = param_part = None

    def send_pieces(first, last, depth=4):
        for k in others:
            parts = [pieces[i][k] for i in range(first, last)]
            part = parts[0] if len(parts) == 1 else jnp.concatenate(parts, axis=1)
            part = send(part, k, depth)
            if chunks[first][0] == "load":
                width = part.shape[1] // (last - first)
                for i in range(first, last):
                    places.append(place_of(i, k))
                    placed.append(part[:, (i - first) * width : (i - first + 1) * width])
            else:
                places.append(place_of(first, k))
                placed.append(part)

    def chunk_done(i):
        nonlocal total
        if i not in own_early:
            x = after(snapshots, held[i - 1][0]) if i else snapshots
            own_early[i] = shares(x, chunks[i], (0,))[0]
        own = own_early[i]
        before, partners = total, held[i]
        last = i == len(chunks) - 1
        if last and i:
            before, partners = after((before, partners), param_part, far)
        out = run_chunk(basis, [own, *partners], before, last)
        cores.append(out[0])
        pieces.append(out[1 : n + 1])
        total = out[n + 1 :] if last else out[n + 1]
        if chunks[i][0] == "tile" and not last:
            far.append(swap(cores[i], "param", 1))
        for_own = pieces[i][0]
        places.append(place_of(i, 0))
        placed.append(for_own)

    def put(core, part, at):
        return lax.dynamic_update_slice(core, part, at)

    def load_part():
        rest = []
        for i in range(n_load):
            tile = jnp.zeros((own_rank, loads, LANES), jnp.float32)
            for where, part in zip(places, placed):
                load, lane = where(me)
                if where(0)[1] == chunks[i][1] * LANES:
                    tile = put(tile, part, (0, load, 0))
            rest.append(tile)
        rest = jnp.concatenate(rest, axis=2)
        other = swap(rest, "param", 1)
        both = jnp.where(
            half == 0,
            jnp.concatenate([rest, other], axis=1),
            jnp.concatenate([other, rest], axis=1),
        )
        return jnp.einsum("rps,rqs->pq", rest, both, precision=precise_mode)

    ahead = 2
    load_sent = n_load == 0
    packs = ()
    own_early = {}
    for i, chunk in enumerate(chunks):
        x = after(snapshots, packs, held[i - 3] if i >= 3 else ())
        packs = parts = shares(x, chunk, others)
        if i == len(chunks) - 1:
            for j in range(max(0, i - ahead + 1), i + 1):
                x = after(snapshots, held[i - 2][0]) if i >= 2 else snapshots
                own_early[j] = shares(x, chunks[j], (0,))[0]
            parts = after(parts, own_early, () if param_part is None else param_part)
        held.append([send(v, k) for v, k in zip(parts, others)])
        if i >= ahead:
            chunk_done(i - ahead)
        if len(cores) == n_load and not load_sent and mains:
            send_pieces(0, n_load, 99)
            load_sent = True
            param_part = load_part()
    for i in range(len(chunks) - ahead, len(chunks)):
        chunk_done(i)
    if not load_sent:
        send_pieces(0, n_load)
        param_part = load_part()
    keep, other_half = total
    wide = -(-total_loads // LANES) * LANES
    steps = n * rows
    across = steps // wide
    fused = mains == 1 and group == 8 and loads * LANES == 8 * steps and n_load
    got = swap(other_half, "param", 1)
    if fused:
        far_last = swap(cores[-1], "param", 1)
        part = load_gram(cores[n_load:], far)
        mixed = fold(keep, got, far_last, part, param_part, cores[n_load:])
    else:
        if mains:
            far.append(swap(cores[-1], "param", 1))
        for m in range(mains):
            these = slice(m * groups, (m + 1) * groups)
            part = load_gram(cores[n_load:][these], far[these])
            swapped = jnp.concatenate([part[:, loads:], part[:, :loads]], axis=1)
            part = jnp.where(half == 0, part, swapped)
            param_part = part if param_part is None else param_part + part
        padded = jnp.pad(param_part, ((0, 0), (0, wide - total_loads)))
        extra = padded.reshape(across, loads // across, wide).swapaxes(0, 1)
        extra = extra.reshape(loads // across, steps)
        rows_part = keep + got
        mixed = [jnp.concatenate([pick(rows_part, k), extra]) for k in range(n)]
    arrived = [send(mixed[k], k) for k in others]
    mine = mixed[0]
    for part in arrived:
        mine = mine + part
    mine = all_sum(mine, "space")

    for m in range(mains):
        at = n_load + m * groups
        send_pieces(at, at + groups)
    if cut % 8 == 0 and group % 8 == 0:
        core = place_pieces(n, places, placed, (own_rank, loads, points))
    else:
        core = jnp.zeros((own_rank, loads, points), jnp.float32)
        for where, part in zip(places, placed):
            core = put(core, part, (0, *where(me)))

    extra = mine[rows // 2 :].reshape(loads // across, across, wide).swapaxes(0, 1)
    gram_param = extra.reshape(loads, wide)[:, :total_loads] / (rank * total_points)
    other = swap(mine, "param", 1)[: rows // 2]
    mine = mine[: rows // 2]
    gram_time = jnp.where(
        half == 0,
        jnp.concatenate([mine, other]),
        jnp.concatenate([other, mine]),
    )
    gram_time = gram_time / (total_loads * total_points)
    return (gram_time, core, gram_param)


def solution(mesh):
    placed = (P("tm", "param", "space"), P())
    return jax.shard_map(
        body,
        mesh=mesh,
        in_specs=placed,
        out_specs=(P("tm", None), P("tm", "param", "space"), P("param", None)),
        check_vma=False,
    )
```
